128 devices in a mesh: dp: 8 (over x, z_lo), seq: 16 (over y, z_hi, core).
Axes of the slice: x: 4, y: 4, z: 4 (z_hi: 2, z_lo: 2; z = z_hi * 2 + z_lo), core: 2. Of those that a mesh axis runs over, the one named last changes fastest.
Arguments:
- inputs: float32 [16, 2048, 1024], P('dp', 'seq'), may hold values from -6 to 6
- w_in: float32 [1024, 3072], P(('dp', 'seq')), may hold values from -0.1875 to 0.1875
- w_out: float32 [1024, 1024], P(('dp', 'seq')), may hold values from -0.1875 to 0.1875
- w_gate: float32 [1024, 4608], P(('dp', 'seq')), may hold values from -0.1875 to 0.1875
- w_up: float32 [1024, 4608], P(('dp', 'seq')), may hold values from -0.1875 to 0.1875
- w_down: float32 [4608, 1024], P(('dp', 'seq')), may hold values from -0.1875 to 0.1875
- conv_weight: float32 [3, 1024], P(None, ('dp', 'seq')), may hold values from -3 to 3
- gain_a: float32 [1024], P(('dp', 'seq')), may hold values from 0.25 to 1.75
- gain_b: float32 [1024], P(('dp', 'seq')), may hold values from 0.25 to 1.75
- cotangent: float32 [16, 2048, 1024], P('dp', 'seq'), may hold values from -6 to 6
Outputs:
- outputs: float32 [16, 2048, 1024], P('dp', 'seq')
- grad_inputs: float32 [16, 2048, 1024], P('dp', 'seq')
- grad_w_in: float32 [1024, 3072], P(('dp', 'seq'))
- grad_w_out: float32 [1024, 1024], P(('dp', 'seq'))
- grad_w_gate: float32 [1024, 4608], P(('dp', 'seq'))
- grad_w_up: float32 [1024, 4608], P(('dp', 'seq'))
- grad_w_down: float32 [4608, 1024], P(('dp', 'seq'))
- grad_conv: float32 [3, 1024], P(None, ('dp', 'seq'))
- grad_gain_a: float32 [1024], P(('dp', 'seq'))
- grad_gain_b: float32 [1024], P(('dp', 'seq'))
The draws below stay inside these ranges and needn't reach their ends.
All inputs are finite; a program needn't handle non-finite values.
Results may differ from the reference program's by a relative error of at most 0.012.
The reference program's roundings to bfloat16 on the way count: a program that leaves them out, or rounds other values in their place, can miss the bound.
Values may be sent and summed in bfloat16 or wider, within the bound.
No kernel may reach another device: no remote copies, remote signals or barrier semaphores. Data moves between devices by JAX's collectives and lax.ppermute only.
A program may use at most 384 MiB of HBM per device.

```python
import jax
import jax.numpy as jnp
from jax import lax

D = 1024
FF = 4608
LEN = 2048
SEQS = 16


def steps_of(key, shape, cuts, smallest, top_value):
    def one(axis_at, shards_of):
        steps = jax.random.uniform(jax.random.fold_in(jax.random.fold_in(key, 6), axis_at), (shards_of,), jnp.float32, smallest / len(cuts), top_value / len(cuts))
        return jnp.repeat(jnp.exp(steps), shape[axis_at] // shards_of).reshape((-1,) + (1,) * (len(shape) - axis_at - 1))

    gain = one(*cuts[0])
    for cut in cuts[1:]:
        gain = gain * one(*cut)
    return gain


def noise(rng, shape, spread, reach, split=(), dtype=jnp.bfloat16):
    factor_of = steps_of(rng, shape, split, -0.22, 0.18) if split else 1.0
    values = jax.random.normal(rng, shape, jnp.float32) * spread * factor_of
    return jnp.minimum(jnp.maximum(values, -reach), reach).astype(dtype)


def setup_inputs(seed: int = 0) -> dict:
    key_list = jax.random.split(jax.random.key(seed), 11)
    return {
        "inputs": noise(key_list[0], (SEQS, LEN, D), 1.0, 6.0, ((0, 8), (1, 16)), jnp.float32),
        "w_in": noise(key_list[1], (D, 3 * D), D ** -0.5, 0.1875, ((0, 128),), jnp.float32),
        "w_out": noise(key_list[2], (D, D), D ** -0.5, 0.1875, ((0, 128),), jnp.float32),
        "w_gate": noise(key_list[3], (D, FF), D ** -0.5, 0.1875, ((0, 128),), jnp.float32),
        "w_up": noise(key_list[4], (D, FF), D ** -0.5, 0.1875, ((0, 128),), jnp.float32),
        "w_down": noise(key_list[5], (FF, D), (FF // 4) ** -0.5, 0.1875, ((0, 128),), jnp.float32),
        "conv_weight": noise(key_list[6], (3, D), 0.6, 3.0, ((1, 128),), jnp.float32),
        "gain_a": jnp.clip(1.0 + 0.15 * jax.random.normal(key_list[7], (D,), jnp.float32), 0.25, 1.75),
        "gain_b": jnp.clip(1.0 + 0.15 * jax.random.normal(key_list[8], (D,), jnp.float32), 0.25, 1.75),
        "cotangent": noise(key_list[9], (SEQS, LEN, D), 1.0, 6.0, ((0, 8), (1, 16)), jnp.float32),
    }


@jax.custom_vjp
def low(v):
    return lax.optimization_barrier(v.astype(jnp.bfloat16)).astype(jnp.float32)

@jax.custom_vjp
def low_back(v):
    return v

def low_keep(v):
    return (low(v), None)

def low_pass(kept, grad):
    return (grad,)

def back_keep(v):
    return (v, None)

def back_low(kept, grad):
    return (low(grad),)
low.defvjp(low_keep, low_pass)
low_back.defvjp(back_keep, back_low)
EPS = 1e-05

def matmul(left, right):
    return jnp.dot(left, right, precision=lax.Precision.HIGHEST, preferred_element_type=jnp.float32)

def forward(params, seq_rows):
    w_in, w_out, w_gate, w_up, w_down, conv_weight, gain_a, gain_b = params
    width = seq_rows.shape[1]
    scale_a = lax.rsqrt(lax.optimization_barrier(jnp.mean(seq_rows * seq_rows, axis=-1, keepdims=True)) + EPS)
    normed = low(seq_rows * scale_a * gain_a)
    projected = low_back(matmul(normed, w_in))
    b_part = projected[:, :width]
    c_part = projected[:, width:2 * width]
    v_part = projected[:, 2 * width:]
    product = b_part * v_part
    padded = jnp.pad(product, ((2, 0), (0, 0)))
    conv_out = conv_weight[0] * padded[:-2] + conv_weight[1] * padded[1:-1] + conv_weight[2] * padded[2:]
    gated = low(c_part * conv_out)
    branch = low_back(matmul(gated, w_out))
    middle = seq_rows + branch
    scale_b = lax.rsqrt(lax.optimization_barrier(jnp.mean(middle * middle, axis=-1, keepdims=True)) + EPS)
    normed_b = low(middle * scale_b * gain_b)
    gate_val = low_back(matmul(normed_b, w_gate))
    up_val = low_back(matmul(normed_b, w_up))
    hidden = low(jax.nn.silu(gate_val) * up_val)
    return middle + low_back(matmul(hidden, w_down))

def reference(inputs, w_in, w_out, w_gate, w_up, w_down, conv_weight, gain_a, gain_b, cotangent):
    params = tuple((low(p) for p in (w_in, w_out, w_gate, w_up, w_down, conv_weight, gain_a, gain_b)))
    zeros = tuple((jnp.zeros(p.shape, jnp.float32) for p in params))

    def one_sequence(totals, pair):
        seq_rows, seq_cot = pair
        result, pullback = jax.vjp(forward, params, seq_rows)
        grad_params, grad_rows = pullback(seq_cot)
        totals = tuple((t + g for t, g in zip(totals, grad_params)))
        return (totals, (result, grad_rows))
    totals, (outputs, grad_inputs) = lax.scan(one_sequence, zeros, (inputs, cotangent))
    return (outputs, grad_inputs, totals[0], totals[1], totals[2], totals[3], totals[4], totals[5], totals[6], totals[7])
```

```python
import jax
import jax.numpy as jnp
from jax import lax
from jax.sharding import Mesh, PartitionSpec as P

AXES = ("x", "zl", "y", "zh", "c")
SIZES = (4, 2, 4, 2, 2)
EPS = 1e-05
bf = jnp.bfloat16
f32 = jnp.float32

RING_AXES = {"x": ("x",), "y": ("y",), "z": ("zl", "zh")}
SLOT = {"x": (0, 1, 2, 3), "y": (0, 1, 2, 3), "z": (0, 2, 1, 3)}
DIMS = {"x": (0,), "y": (2,), "z": (1, 3)}


def swap(value):
    return lax.ppermute(value, "c", [(0, 1), (1, 0)])


def rotate(value, ring, steps):
    slot = SLOT[ring]
    return lax.ppermute(
        value, RING_AXES[ring], [(slot[i], slot[(i + steps) % 4]) for i in range(4)]
    )


def pass_on(value, ring):
    slot = SLOT[ring]
    pairs = []
    for i in range(4):
        pairs.append((2 * slot[i], 2 * slot[(i + 1) % 4]))
        pairs.append((2 * slot[i] + 1, 2 * slot[(i - 1) % 4] + 1))
    return lax.ppermute(value, (*RING_AXES[ring], "c"), pairs)


def trade_halves(value):
    return lax.ppermute(
        value, ("x", "c"), [(0, 0), (1, 4), (2, 2), (3, 6), (4, 1), (5, 5), (6, 3), (7, 7)]
    )


def place(ring):
    if ring == "z":
        return 2 * lax.axis_index("zh") + lax.axis_index("zl")
    return lax.axis_index(ring)


def start_at(ring, position, rank):
    at = [0] * rank
    if ring == "z":
        at[1], at[3] = lax.rem(position, 2), lax.div(position, 2)
    else:
        at[DIMS[ring][0]] = position
    return at


def upstream(ring, steps):
    core = lax.axis_index("c")
    return lax.rem(place(ring) + jnp.where(core == 0, 4 - steps, steps), 4)


def put_blocks(blocks, positions, ring):
    shape = list(blocks[0].shape)
    for d in DIMS[ring]:
        shape[d] = 4 // len(DIMS[ring])
    out = jnp.zeros(shape, blocks[0].dtype)
    for block, position in zip(blocks, positions):
        out = lax.dynamic_update_slice(out, block, start_at(ring, position, out.ndim))
    return out


def gather_direct(value, ring):
    blocks = [value] + [rotate(value, ring, k) for k in (1, 2, 3)]
    here = place(ring)
    return put_blocks(blocks, [lax.rem(here + 4 - k, 4) for k in range(4)], ring)


def gather_ring(value, ring):
    blocks = [value]
    for _ in range(3):
        blocks.append(pass_on(blocks[-1], ring))
    return put_blocks(blocks, [upstream(ring, k) for k in range(4)], ring)


def block_of(array, ring, position):
    shape = list(array.shape)
    for d in DIMS[ring]:
        shape[d] = 1
    return lax.dynamic_slice(array, start_at(ring, position, array.ndim), shape)


def sum_ring(array, ring):
    total = block_of(array, ring, upstream(ring, 1))
    for k in (2, 3, 0):
        arrived = pass_on(total, ring)
        mine = block_of(array, ring, upstream(ring, k))
        total = (arrived.astype(f32) + mine.astype(f32)).astype(bf)
    return total


def sum_direct(array, ring):
    here = place(ring)
    total = block_of(array, ring, here).astype(f32)
    for k in (1, 2, 3):
        sent = block_of(array, ring, lax.rem(here + k, 4))
        total = total + rotate(sent, ring, k).astype(f32)
    return total


def matmul(left, right):
    return jnp.dot(left, right, preferred_element_type=f32)


def outer_sum(left, right):
    return lax.dot_general(
        left, right, (((0,), (0,)), ((), ())), preferred_element_type=f32
    )


def times_transpose(grad, weight):
    return lax.dot_general(
        grad, weight, (((1,), (1,)), ((), ())), preferred_element_type=f32
    )


def local(inputs, w_in, w_out, w_gate, w_up, w_down, conv_weight, gain_a, gain_b, cotangent):
    groups, tokens, width = inputs.shape
    rows = groups * tokens
    hidden = w_gate.shape[1] // 2
    half = width // 2
    quarter = half // 2
    core = lax.axis_index("c")
    first = core == 0

    def in_order(mine, other, axis):
        return jnp.where(
            first,
            jnp.concatenate([mine, other], axis=axis),
            jnp.concatenate([other, mine], axis=axis),
        )

    x_own = inputs.reshape(rows, width)
    g_own = cotangent.reshape(rows, width)
    x_all = jnp.concatenate([x_own, swap(x_own)], axis=0)
    df_own = g_own.astype(bf)
    d_out = jnp.concatenate([df_own, swap(df_own)], axis=0)

    params = jnp.concatenate(
        [gain_a[:, None], gain_b[:, None], conv_weight.T, jnp.zeros((8, 123), f32)], axis=1
    )

    def columns(side):
        def cut(w, at, size):
            return lax.dynamic_slice_in_dim(w, at, size, 1)

        return jnp.concatenate(
            [
                cut(w_gate, side * hidden, hidden),
                cut(w_in, side * half, half),
                cut(w_in, 2 * width + side * half, quarter),
                params,
                cut(w_up, side * hidden, hidden),
                cut(w_in, width + side * half, half),
                cut(w_in, 2 * width + side * half + quarter, quarter),
            ],
            axis=1,
        ).astype(bf)

    shard = in_order(columns(core), swap(columns(1 - core)), 0)
    x_cols = hidden + half + quarter + 128
    x_shard = shard[None, None, None, None, :, :x_cols]
    y_shard = shard[None, None, None, None, :, x_cols:]
    d_shard = trade_halves(jnp.concatenate([w_down, w_out], axis=0).astype(bf))
    n_down, n_out = w_down.shape[0], w_out.shape[0]

    x_part = gather_direct(gather_direct(x_shard, "z"), "y")
    y_part = gather_direct(gather_direct(y_shard, "y"), "x")
    d_part = gather_direct(d_shard[None, None, None, None], "x")

    def pair_up(a):
        a = a.reshape(2, 2, a.shape[-2], width).transpose(1, 0, 2, 3)
        return a.reshape(2, 1, 1, 1, -1, width)

    d_part = jnp.concatenate(
        [pair_up(d_part[..., :n_down, :]), pair_up(d_part[..., n_down:, :])], axis=4
    )
    d_part = gather_direct(d_part, "z")

    x_one = gather_ring(x_part[..., hidden:], "x").reshape(width, -1)
    y_one = gather_ring(y_part[..., hidden:], "z").reshape(width, -1)
    full_out = gather_ring(d_part[..., 2 * n_down :, :], "y").reshape(half, width)
    full_gate = gather_ring(x_part[..., :hidden], "x").reshape(width, hidden)
    full_up = gather_ring(y_part[..., :hidden], "z").reshape(width, hidden)
    full_down = gather_ring(d_part[..., : 2 * n_down, :], "y").reshape(hidden, width)

    in_x = x_one[:, : half + quarter]
    in_y = y_one
    vectors = x_one[:, half + quarter :].astype(f32).T
    ga, gb = vectors[0], vectors[1]
    taps = lax.dynamic_slice_in_dim(vectors[2:5], core * half, half, 1)

    scale_a = lax.rsqrt(jnp.mean(x_all * x_all, axis=-1, keepdims=True) + EPS)
    normed = (x_all * scale_a * ga).astype(bf)
    proj_x = matmul(normed, in_x)
    proj_y = matmul(normed, in_y)
    b_part, c_part = proj_x[:, :half], proj_y[:, :half]
    v_part = jnp.concatenate([proj_x[:, half:], proj_y[:, half:]], axis=1)
    product = (b_part * v_part).reshape(2, groups, tokens, half)

    def along_sequence(value, steps):
        chips = 8
        return lax.ppermute(
            value,
            ("y", "zh"),
            [(i, i + steps) for i in range(chips) if 0 <= i + steps < chips],
        )

    tail_own, tail_other = product[0, :, tokens - 2 :], product[1, :, tokens - 2 :]
    halo = along_sequence(jnp.where(first, tail_other, tail_own), 1)
    before = jnp.stack(
        [jnp.where(first, halo, tail_other), jnp.where(first, tail_own, halo)]
    )
    extended = jnp.concatenate([before, product], axis=2)
    conv_out = (
        taps[0] * extended[:, :, :-2] + taps[1] * extended[:, :, 1:-1] + taps[2] * extended[:, :, 2:]
    ).reshape(2 * rows, half)
    gated = (c_part * conv_out).astype(bf)

    def sum_cores(partial):
        return partial[:rows] + swap(partial[rows:])

    middle = x_own + sum_cores(matmul(gated, full_out))
    scale_b = lax.rsqrt(jnp.mean(middle * middle, axis=-1, keepdims=True) + EPS)
    normed_b_own = (middle * scale_b * gb).astype(bf)
    normed_b = jnp.concatenate([normed_b_own, swap(normed_b_own)], axis=0)
    gate_val = matmul(normed_b, full_gate)
    up_val = matmul(normed_b, full_up)
    sigma = jax.nn.sigmoid(gate_val)
    swish = gate_val * sigma
    hidden_val = (swish * up_val).astype(bf)
    outputs = middle + sum_cores(matmul(hidden_val, full_down))

    grad_w_down = outer_sum(hidden_val, d_out).astype(bf)
    d_hidden = times_transpose(d_out, full_down)
    d_gate = (d_hidden * up_val * sigma * (1.0 + gate_val * (1.0 - sigma))).astype(bf)
    d_up = (d_hidden * swish).astype(bf)
    grad_w_gate = outer_sum(normed_b, d_gate).astype(bf)
    grad_w_up = outer_sum(normed_b, d_up).astype(bf)

    chips = (4, 2, 4, 2)
    x_two = sum_ring(grad_w_gate.reshape(*chips, 16, hidden), "x")
    y_two = sum_ring(grad_w_up.reshape(*chips, 16, hidden), "z")
    d_two = sum_ring(grad_w_down.reshape(2, 2, 4, 2, 2 * n_down, width), "y")

    d_normed_b = sum_cores(times_transpose(d_gate, full_gate) + times_transpose(d_up, full_up))
    grad_gain_b = jnp.sum(d_normed_b * middle * scale_b, axis=0)
    scaled_b = d_normed_b * gb
    d_middle = (
        g_own
        + scale_b * scaled_b
        - middle * scale_b**3 * jnp.mean(scaled_b * middle, axis=-1, keepdims=True)
    )
    d_branch_own = d_middle.astype(bf)
    d_branch = jnp.concatenate([d_branch_own, swap(d_branch_own)], axis=0)
    grad_w_out = outer_sum(gated, d_branch).astype(bf)
    d_gated = times_transpose(d_branch, full_out)
    d_c = d_gated * conv_out
    d_conv = (d_gated * c_part).reshape(2, groups, tokens, half)
    head_own, head_other = d_conv[0, :, :2], d_conv[1, :, :2]
    halo_b = along_sequence(jnp.where(first, head_own, head_other), -1)
    after = jnp.stack(
        [jnp.where(first, head_other, halo_b), jnp.where(first, halo_b, head_own)]
    )
    ext_b = jnp.concatenate([d_conv, after], axis=2)
    d_product = (
        taps[0] * ext_b[:, :, 2:] + taps[1] * ext_b[:, :, 1:-1] + taps[2] * ext_b[:, :, :-2]
    ).reshape(2 * rows, half)
    grad_taps = jnp.stack(
        [jnp.sum(d_conv * extended[:, :, k : k + tokens], axis=(0, 1, 2)) for k in range(3)]
    )
    d_v = d_product * b_part
    d_x = jnp.concatenate([d_product * v_part, d_v[:, :quarter]], axis=1).astype(bf)
    d_y = jnp.concatenate([d_c, d_v[:, quarter:]], axis=1).astype(bf)
    grad_in_x = outer_sum(normed, d_x).astype(bf)
    grad_in_y = outer_sum(normed, d_y).astype(bf)
    d_normed_part = times_transpose(d_x, in_x) + times_transpose(d_y, in_y)
    grad_gain_a = jnp.sum(d_normed_part * x_all * scale_a, axis=0)
    d_normed = sum_cores(d_normed_part)
    scale_own = scale_a[:rows]
    scaled_a = d_normed * ga
    grad_rows = (
        d_middle
        + scale_own * scaled_a
        - x_own * scale_own**3 * jnp.mean(scaled_a * x_own, axis=-1, keepdims=True)
    )

    both_taps = lax.dynamic_update_slice(jnp.zeros((3, width), f32), grad_taps, (0, core * half))
    grad_vectors = jnp.concatenate(
        [grad_gain_a[None], grad_gain_b[None], both_taps, jnp.zeros((123, width), f32)], axis=0
    ).astype(bf)
    grad_x_one = jnp.concatenate([grad_in_x, grad_vectors.T], axis=1)
    x_one_sum = sum_ring(grad_x_one.reshape(*chips, 16, -1), "x")
    y_one_sum = sum_ring(grad_in_y.reshape(*chips, 16, -1), "z")
    d_one_sum = sum_ring(grad_w_out.reshape(2, 2, 4, 2, 2 * n_out, width), "y")

    x_sum = sum_direct(jnp.concatenate([x_two, x_one_sum], axis=-1), "y").astype(bf)
    x_sum = sum_direct(x_sum, "z")
    y_sum = sum_direct(jnp.concatenate([y_two, y_one_sum], axis=-1), "x").astype(bf)
    y_sum = sum_direct(y_sum, "y")
    d_sum = sum_direct(jnp.concatenate([d_two, d_one_sum], axis=-2), "z").astype(bf)

    def unpair(a):
        a = a.reshape(2, 2, -1, width).transpose(1, 0, 2, 3)
        return a.reshape(4, 1, 1, 1, -1, width)

    d_sum = jnp.concatenate(
        [unpair(d_sum[..., : 2 * n_down, :]), unpair(d_sum[..., 2 * n_down :, :])], axis=4
    )
    d_sum = trade_halves(sum_direct(d_sum, "x").reshape(n_down + n_out, width))

    sums = jnp.concatenate([x_sum, y_sum], axis=-1).reshape(16, -1)
    mine = lax.dynamic_slice_in_dim(sums, core * 8, 8, 0)
    other = swap(lax.dynamic_slice_in_dim(sums, (1 - core) * 8, 8, 0))

    def cut(a, at, size):
        return a[:, at : at + size]

    def joined(at, size):
        return in_order(cut(mine, at, size), cut(other, at, size), 1)

    at_v1, at_vec = hidden + half, hidden + half + quarter
    at_up, at_c, at_v2 = x_cols, x_cols + hidden, x_cols + hidden + half
    v_mine = jnp.concatenate([cut(mine, at_v1, quarter), cut(mine, at_v2, quarter)], axis=1)
    v_other = jnp.concatenate([cut(other, at_v1, quarter), cut(other, at_v2, quarter)], axis=1)
    grad_w_in = jnp.concatenate(
        [joined(hidden, half), joined(at_c, half), in_order(v_mine, v_other, 1)], axis=1
    )
    vec = (cut(mine, at_vec, 128) + cut(other, at_vec, 128))[:, :5].T
    return (
        outputs.reshape(groups, tokens, width),
        grad_rows.reshape(groups, tokens, width),
        grad_w_in,
        d_sum[n_down:],
        joined(0, hidden),
        joined(at_up, hidden),
        d_sum[:n_down],
        vec[2:5],
        vec[0],
        vec[1],
    )


def solution(mesh):
    fine = Mesh(mesh.devices.reshape(SIZES), AXES)
    dp, seq = ("x", "zl"), ("y", "zh", "c")
    tokens = P(dp, seq, None)
    by_row = P(AXES, None)
    vector = P(AXES)
    taps = P(None, AXES)
    return jax.shard_map(
        local,
        mesh=fine,
        in_specs=(
            tokens, by_row, by_row, by_row, by_row, by_row, taps, vector, vector, tokens,
        ),
        out_specs=(
            tokens, tokens, by_row, by_row, by_row, by_row, by_row, taps, vector, vector,
        ),
        check_vma=False,
    )
```

```python
import jax
import jax.numpy as jnp
from jax import lax
from jax.experimental import pallas as pl
from jax.experimental.pallas import tpu as pltpu
from jax.sharding import Mesh, PartitionSpec as P

AXES = ("x", "zl", "y", "zh", "c")
SIZES = (4, 2, 4, 2, 2)
EPS = 1e-05
bf = jnp.bfloat16
f32 = jnp.float32

RING_AXES = {"x": ("x",), "y": ("y",), "z": ("zl", "zh")}
SLOT = {"x": (0, 1, 2, 3), "y": (0, 1, 2, 3), "z": (0, 2, 1, 3)}
DIMS = {"x": (0,), "y": (2,), "z": (1, 3)}


def swap(value):
    return lax.ppermute(value, "c", [(0, 1), (1, 0)])


def partner(value, ring, step):
    slot = SLOT[ring]
    masks = (1, 3) if step == 0 else (3, 1)
    pairs = [(2 * slot[i] + c, 2 * slot[i ^ masks[c]] + c) for i in range(4) for c in range(2)]
    return lax.ppermute(value, (*RING_AXES[ring], "c"), pairs)


def trade_halves(value):
    return lax.ppermute(
        value, ("x", "c"), [(0, 0), (1, 4), (2, 2), (3, 6), (4, 1), (5, 5), (6, 3), (7, 7)]
    )


def place(ring):
    if ring == "z":
        return 2 * lax.axis_index("zh") + lax.axis_index("zl")
    return lax.axis_index(ring)


def start_at(ring, position, rank):
    at = [0] * rank
    if ring == "z":
        at[1], at[3] = lax.rem(position, 2), lax.div(position, 2)
    else:
        at[DIMS[ring][0]] = position
    return at


def positions(ring):
    here = place(ring)
    odd = lax.axis_index("c") * 2
    return here, here ^ (1 + odd), here ^ (3 - odd), here ^ 2


def put_blocks(blocks, positions, ring):
    shape = list(blocks[0].shape)
    for d in DIMS[ring]:
        shape[d] = 4 // len(DIMS[ring])
    out = jnp.zeros(shape, blocks[0].dtype)
    for block, position in zip(blocks, positions):
        out = lax.dynamic_update_slice(out, block, start_at(ring, position, out.ndim))
    return out


def gather(values, rings):
    near = [partner(v, r, 0) for v, r in zip(values, rings)]
    twos = [partner(jnp.stack([v, n]), r, 1) for v, n, r in zip(values, near, rings)]
    return [
        put_blocks([v, n, t[0], t[1]], positions(r), r)
        for v, n, t, r in zip(values, near, twos, rings)
    ]


def gather_wide_start(values, rings):
    near = [partner(v, r, 0) for v, r in zip(values, rings)]
    across = [partner(v, r, 1) for v, r in zip(values, rings)]
    return near, across


def gather_wide_end(values, rings, near, across):
    far = [partner(n, r, 1) for n, r in zip(near, rings)]
    return [
        put_blocks([v, n, a, f], positions(r), r)
        for v, n, a, f, r in zip(values, near, across, far, rings)
    ]


def block_of(array, ring, position):
    shape = list(array.shape)
    for d in DIMS[ring]:
        shape[d] = 1
    return lax.dynamic_slice(array, start_at(ring, position, array.ndim), shape)


def blocks_of(array, ring):
    own, near, across, far = (block_of(array, ring, p) for p in positions(ring))
    return own, near, jnp.stack([across, far])


def sum_start(blocks, rings):
    return [partner(v[2], r, 1) for v, r in zip(blocks, rings)]


def sum_middle(blocks, rings, twos):
    return [
        partner((v[1].astype(f32) + t[1].astype(f32)).astype(bf), r, 0)
        for v, r, t in zip(blocks, rings, twos)
    ]


def sum_end(blocks, twos, ones):
    return [
        v[0].astype(f32) + t[0].astype(f32) + n.astype(f32) for v, t, n in zip(blocks, twos, ones)
    ]


def sum_over(arrays, rings):
    blocks = [blocks_of(v, r) for v, r in zip(arrays, rings)]
    twos = sum_start(blocks, rings)
    return sum_end(blocks, twos, sum_middle(blocks, rings, twos))


def matmul(left, right):
    return jnp.dot(left, right, preferred_element_type=f32)


def outer_sum(left, right):
    return lax.dot_general(
        left, right, (((0,), (0,)), ((), ())), preferred_element_type=f32
    )


def times_transpose(grad, weight):
    return lax.dot_general(
        grad, weight, (((1,), (1,)), ((), ())), preferred_element_type=f32
    )


def feed_forward_kernel(
    h_ref, hg_ref, hu_ref, g_ref, wg_ref, wu_ref, wd_ref, out_ref, dh_ref, gd_ref, *grad_refs
):
    @pl.when(pl.program_id(0) == 0)
    def _():
        out_ref[...] = jnp.zeros_like(out_ref)
        dh_ref[...] = jnp.zeros_like(dh_ref)

    h, g, wg, wu, wd = h_ref[...], g_ref[...], wg_ref[...], wu_ref[...], wd_ref[...]
    gate = matmul(h, wg)
    up = matmul(h, wu)
    d_hidden = times_transpose(g, wd)
    sigma = jax.nn.sigmoid(gate)
    swish = gate * sigma
    hidden = (swish * up).astype(bf)
    d_gate = (d_hidden * up * sigma * (1.0 + gate * (1.0 - sigma))).astype(bf)
    d_up = (d_hidden * swish).astype(bf)
    gd_ref[...] = outer_sum(hidden, g).astype(bf)
    block = hg_ref.shape[0] // 4
    for h_turned, grad, refs in ((hg_ref, d_gate, grad_refs[:2]), (hu_ref, d_up, grad_refs[2:])):
        for k in range(4):
            part = matmul(h_turned[k * block : (k + 1) * block], grad)
            refs[k // 2][k % 2] = part.astype(bf)
    out_ref[...] += matmul(hidden, wd)
    dh_ref[...] += times_transpose(d_gate, wg) + times_transpose(d_up, wu)


def feed_forward(h, h_gate, h_up, g, wg, wu, wd):
    rows, width = h.shape
    hidden, tile = wg.shape[1], 256
    whole = pl.BlockSpec((rows, width), lambda i: (0, 0))
    turned = pl.BlockSpec((width, rows), lambda i: (0, 0))
    columns = pl.BlockSpec((width, tile), lambda i: (0, i))
    blocks = pl.BlockSpec((2, width // 4, tile), lambda i: (0, 0, i))
    down = pl.BlockSpec((tile, width), lambda i: (i, 0))
    return pl.pallas_call(
        feed_forward_kernel,
        grid=(hidden // tile,),
        in_specs=[whole, turned, turned, whole, columns, columns, down],
        out_specs=[whole, whole, down] + [blocks] * 4,
        out_shape=[
            jax.ShapeDtypeStruct((rows, width), f32),
            jax.ShapeDtypeStruct((rows, width), f32),
            jax.ShapeDtypeStruct((hidden, width), bf),
        ]
        + [jax.ShapeDtypeStruct((2, width // 4, hidden), bf)] * 4,
        compiler_params=pltpu.CompilerParams(
            dimension_semantics=("arbitrary",), vmem_limit_bytes=48 * 1024 * 1024
        ),
        cost_estimate=pl.CostEstimate(
            flops=18 * rows * width * hidden,
            bytes_accessed=12 * width * hidden + 16 * rows * width,
            transcendentals=rows * hidden,
        ),
    )(h, h_gate, h_up, g, wg, wu, wd)


def local(inputs, w_in, w_out, w_gate, w_up, w_down, conv_weight, gain_a, gain_b, cotangent):
    groups, tokens, width = inputs.shape
    rows = groups * tokens
    hidden = w_gate.shape[1] // 2
    half = width // 2
    quarter = half // 2
    core = lax.axis_index("c")
    first = core == 0

    def in_order(mine, other, axis):
        return jnp.where(
            first,
            jnp.concatenate([mine, other], axis=axis),
            jnp.concatenate([other, mine], axis=axis),
        )

    x_own = inputs.reshape(rows, width)
    g_own = cotangent.reshape(rows, width)
    x_all = jnp.concatenate([x_own, swap(x_own)], axis=0)
    df_own = g_own.astype(bf)
    d_out = jnp.concatenate([df_own, swap(df_own)], axis=0)

    params = jnp.concatenate(
        [gain_a[:, None], gain_b[:, None], conv_weight.T, jnp.zeros((8, 123), f32)], axis=1
    )

    def columns(side):
        def cut(w, at, size):
            return lax.dynamic_slice_in_dim(w, at, size, 1)

        return jnp.concatenate(
            [
                cut(w_gate, side * hidden, hidden),
                cut(w_in, side * half, half),
                cut(w_in, 2 * width + side * half, quarter),
                params,
                cut(w_up, side * hidden, hidden),
                cut(w_in, width + side * half, half),
                cut(w_in, 2 * width + side * half + quarter, quarter),
            ],
            axis=1,
        ).astype(bf)

    shard = in_order(columns(core), swap(columns(1 - core)), 0)
    x_cols = hidden + half + quarter + 128
    x_shard = shard[None, None, None, None, :, :x_cols]
    y_shard = shard[None, None, None, None, :, x_cols:]
    d_shard = trade_halves(jnp.concatenate([w_down, w_out], axis=0).astype(bf))
    n_down, n_out = w_down.shape[0], w_out.shape[0]

    x_part, y_part, d_part = gather(
        [x_shard, y_shard, d_shard[None, None, None, None]], ["z", "y", "x"]
    )

    def pair_up(a):
        a = a.reshape(2, 2, a.shape[-2], width).transpose(1, 0, 2, 3)
        return a.reshape(2, 1, 1, 1, -1, width)

    d_part = jnp.concatenate(
        [pair_up(d_part[..., :n_down, :]), pair_up(d_part[..., n_down:, :])], axis=4
    )
    x_part, y_part, d_part, x_all, d_out = lax.optimization_barrier(
        (x_part, y_part, d_part, x_all, d_out)
    )
    x_part, y_part, d_part = gather([x_part, y_part, d_part], ["y", "x", "z"])
    x_part, y_part, d_part = lax.optimization_barrier((x_part, y_part, d_part))

    last = ["x", "z", "y"]
    ones = [x_part[..., hidden:], y_part[..., hidden:], d_part[..., 2 * n_down :, :]]
    near_one, across_one = gather_wide_start(ones, last)
    near_one, across_one = lax.optimization_barrier((near_one, across_one))
    ones = gather_wide_end(ones, last, near_one, across_one)
    twos = (x_part[..., :hidden], y_part[..., :hidden], d_part[..., : 2 * n_down, :])
    twos, near_one, across_one = lax.optimization_barrier((twos, near_one, across_one))
    near_two, across_two = gather_wide_start(twos, last)
    x_one, y_one = ones[0].reshape(width, -1), ones[1].reshape(width, -1)
    full_out = ones[2].reshape(half, width)
    in_x = x_one[:, : half + quarter]
    in_y = y_one
    vectors = x_one[:, half + quarter :].astype(f32).T
    ga, gb = vectors[0], vectors[1]
    taps = lax.dynamic_slice_in_dim(vectors[2:5], core * half, half, 1)

    scale_a = lax.rsqrt(jnp.mean(x_all * x_all, axis=-1, keepdims=True) + EPS)
    normed = (x_all * scale_a * ga).astype(bf)
    proj_x = matmul(normed, in_x)
    proj_y = matmul(normed, in_y)
    b_part, c_part = proj_x[:, :half], proj_y[:, :half]
    v_part = jnp.concatenate([proj_x[:, half:], proj_y[:, half:]], axis=1)
    product = (b_part * v_part).reshape(2, groups, tokens, half)

    def along_sequence(value, steps):
        chips = 8
        return lax.ppermute(
            value,
            ("y", "zh"),
            [(i, i + steps) for i in range(chips) if 0 <= i + steps < chips],
        )

    tail_own, tail_other = product[0, :, tokens - 2 :], product[1, :, tokens - 2 :]
    halo = along_sequence(jnp.where(first, tail_other, tail_own), 1)
    before = jnp.stack(
        [jnp.where(first, halo, tail_other), jnp.where(first, tail_own, halo)]
    )
    extended = jnp.concatenate([before, product], axis=2)
    conv_out = (
        taps[0] * extended[:, :, :-2] + taps[1] * extended[:, :, 1:-1] + taps[2] * extended[:, :, 2:]
    ).reshape(2 * rows, half)
    gated = (c_part * conv_out).astype(bf)
    gated, near_two = lax.optimization_barrier((gated, near_two))
    twos = gather_wide_end(twos, last, near_two, across_two)
    full_gate, full_up = twos[0].reshape(width, hidden), twos[1].reshape(width, hidden)
    full_down = twos[2].reshape(hidden, width)


    def sum_cores(partial):
        return partial[:rows] + swap(partial[rows:])

    middle = x_own + sum_cores(matmul(gated, full_out))
    scale_b = lax.rsqrt(jnp.mean(middle * middle, axis=-1, keepdims=True) + EPS)
    normed_b_own = (middle * scale_b * gb).astype(bf)
    normed_b = jnp.concatenate([normed_b_own, swap(normed_b_own)], axis=0)
    chips = (4, 2, 4, 2)
    turned = normed_b.T.reshape(*chips, 16, 2 * rows)
    h_gate, h_up = (
        jnp.concatenate([block_of(turned, r, p).reshape(-1, 2 * rows) for p in positions(r)])
        for r in last[:2]
    )
    out_part, dh_part, grad_w_down, gate_keep, gate_send, up_keep, up_send = feed_forward(
        normed_b, h_gate, h_up, d_out, full_gate, full_up, full_down
    )

    gate_keep, gate_send = (v.reshape(2, 1, 2, 4, 2, 16, hidden) for v in (gate_keep, gate_send))
    up_keep, up_send = (v.reshape(2, 4, 1, 4, 1, 16, hidden) for v in (up_keep, up_send))
    grads_two = [
        (gate_keep[0], gate_keep[1], gate_send),
        (up_keep[0], up_keep[1], up_send),
        blocks_of(grad_w_down.reshape(2, 2, 4, 2, 2 * n_down, width), "y"),
    ]
    arrived_two = sum_start(grads_two, last)

    d_normed_b = sum_cores(dh_part)
    grad_gain_b = jnp.sum(d_normed_b * middle * scale_b, axis=0)
    scaled_b = d_normed_b * gb
    d_middle = (
        g_own
        + scale_b * scaled_b
        - middle * scale_b**3 * jnp.mean(scaled_b * middle, axis=-1, keepdims=True)
    )
    d_branch_own = d_middle.astype(bf)
    d_branch = jnp.concatenate([d_branch_own, swap(d_branch_own)], axis=0)
    grad_w_out = outer_sum(gated, d_branch).astype(bf)
    d_gated = times_transpose(d_branch, full_out)
    d_c = d_gated * conv_out
    d_conv = (d_gated * c_part).reshape(2, groups, tokens, half)
    head_own, head_other = d_conv[0, :, :2], d_conv[1, :, :2]
    halo_b = along_sequence(jnp.where(first, head_own, head_other), -1)
    after = jnp.stack(
        [jnp.where(first, head_other, halo_b), jnp.where(first, halo_b, head_own)]
    )
    ext_b = jnp.concatenate([d_conv, after], axis=2)
    d_product = (
        taps[0] * ext_b[:, :, 2:] + taps[1] * ext_b[:, :, 1:-1] + taps[2] * ext_b[:, :, :-2]
    ).reshape(2 * rows, half)
    grad_taps = jnp.stack(
        [jnp.sum(d_conv * extended[:, :, k : k + tokens], axis=(0, 1, 2)) for k in range(3)]
    )
    d_v = d_product * b_part
    d_x = jnp.concatenate([d_product * v_part, d_v[:, :quarter]], axis=1).astype(bf)
    d_y = jnp.concatenate([d_c, d_v[:, quarter:]], axis=1).astype(bf)
    d_x, d_y, arrived_two = lax.optimization_barrier((d_x, d_y, arrived_two))
    arrived_one = sum_middle(grads_two, last, arrived_two)
    grad_in_x = outer_sum(normed, d_x).astype(bf)
    grad_in_y = outer_sum(normed, d_y).astype(bf)
    d_normed_part = times_transpose(d_x, in_x) + times_transpose(d_y, in_y)
    grad_gain_a = jnp.sum(d_normed_part * x_all * scale_a, axis=0)
    d_normed = sum_cores(d_normed_part)
    scale_own = scale_a[:rows]
    scaled_a = d_normed * ga
    grad_rows = (
        d_middle
        + scale_own * scaled_a
        - x_own * scale_own**3 * jnp.mean(scaled_a * x_own, axis=-1, keepdims=True)
    )

    both_taps = lax.dynamic_update_slice(jnp.zeros((3, width), f32), grad_taps, (0, core * half))
    grad_vectors = jnp.concatenate(
        [grad_gain_a[None], grad_gain_b[None], both_taps, jnp.zeros((123, width), f32)], axis=0
    ).astype(bf)
    grad_x_one = jnp.concatenate([grad_in_x, grad_vectors.T], axis=1)
    grads_one = [
        grad_x_one.reshape(*chips, 16, -1),
        grad_in_y.reshape(*chips, 16, -1),
        grad_w_out.reshape(2, 2, 4, 2, 2 * n_out, width),
    ]
    sums_two = sum_end(grads_two, arrived_two, arrived_one)
    sums_one = sum_over(grads_one, last)
    x_sum, y_sum, d_sum = sum_over(
        [
            jnp.concatenate(v, axis=a).astype(bf)
            for *v, a in zip(sums_two, sums_one, (-1, -1, -2))
        ],
        ["y", "x", "z"],
    )

    def unpair(a):
        a = a.reshape(2, 2, -1, width).transpose(1, 0, 2, 3)
        return a.reshape(4, 1, 1, 1, -1, width)

    d_sum = jnp.concatenate(
        [unpair(d_sum[..., : 2 * n_down, :]), unpair(d_sum[..., 2 * n_down :, :])], axis=4
    )
    x_sum, y_sum, d_sum = sum_over(
        [x_sum.astype(bf), y_sum.astype(bf), d_sum.astype(bf)], ["z", "y", "x"]
    )
    d_sum = trade_halves(d_sum.reshape(n_down + n_out, width))

    sums = jnp.concatenate([x_sum.reshape(16, -1), y_sum.reshape(16, -1)], axis=-1)
    mine = lax.dynamic_slice_in_dim(sums, core * 8, 8, 0)
    other = swap(lax.dynamic_slice_in_dim(sums, (1 - core) * 8, 8, 0))

    def cut(a, at, size):
        return a[:, at : at + size]

    def joined(at, size):
        return in_order(cut(mine, at, size), cut(other, at, size), 1)

    at_v1, at_vec = hidden + half, hidden + half + quarter
    at_up, at_c, at_v2 = x_cols, x_cols + hidden, x_cols + hidden + half
    v_mine = jnp.concatenate([cut(mine, at_v1, quarter), cut(mine, at_v2, quarter)], axis=1)
    v_other = jnp.concatenate([cut(other, at_v1, quarter), cut(other, at_v2, quarter)], axis=1)
    grad_w_in = jnp.concatenate(
        [joined(hidden, half), joined(at_c, half), in_order(v_mine, v_other, 1)], axis=1
    )
    vec = (cut(mine, at_vec, 128) + cut(other, at_vec, 128))[:, :5].T
    outputs = middle + sum_cores(out_part)
    return (
        outputs.reshape(groups, tokens, width),
        grad_rows.reshape(groups, tokens, width),
        grad_w_in,
        d_sum[n_down:],
        joined(0, hidden),
        joined(at_up, hidden),
        d_sum[:n_down],
        vec[2:5],
        vec[0],
        vec[1],
    )


def solution(mesh):
    fine = Mesh(mesh.devices.reshape(SIZES), AXES)
    dp, seq = ("x", "zl"), ("y", "zh", "c")
    tokens = P(dp, seq, None)
    by_row = P(AXES, None)
    vector = P(AXES)
    taps = P(None, AXES)
    return jax.shard_map(
        local,
        mesh=fine,
        in_specs=(
            tokens, by_row, by_row, by_row, by_row, by_row, taps, vector, vector, tokens,
        ),
        out_specs=(
            tokens, tokens, by_row, by_row, by_row, by_row, by_row, taps, vector, vector,
        ),
        check_vma=False,
    )
```

```python
import jax
import jax.numpy as jnp
from jax import lax
from jax.experimental import pallas as pl
from jax.experimental.pallas import tpu as pltpu
from jax.sharding import Mesh, PartitionSpec as P

AXES = ("x", "zl", "y", "zh", "c")
SIZES = (4, 2, 4, 2, 2)
EPS = 1e-05
bf = jnp.bfloat16
f32 = jnp.float32

RING_AXES = {"x": ("x",), "y": ("y",), "z": ("zl", "zh")}
SLOT = {"x": (0, 1, 2, 3), "y": (0, 1, 2, 3), "z": (0, 2, 1, 3)}
DIMS = {"x": (0,), "y": (2,), "z": (1, 3)}


def swap(value):
    return lax.ppermute(value, "c", [(0, 1), (1, 0)])


def partner(value, ring, step):
    slot = SLOT[ring]
    masks = (1, 3) if step == 0 else (3, 1)
    pairs = [(2 * slot[i] + c, 2 * slot[i ^ masks[c]] + c) for i in range(4) for c in range(2)]
    return lax.ppermute(value, (*RING_AXES[ring], "c"), pairs)


def trade_halves(value):
    return lax.ppermute(
        value, ("x", "c"), [(0, 0), (1, 4), (2, 2), (3, 6), (4, 1), (5, 5), (6, 3), (7, 7)]
    )


def place(ring):
    if ring == "z":
        return 2 * lax.axis_index("zh") + lax.axis_index("zl")
    return lax.axis_index(ring)


def start_at(ring, position, rank):
    at = [0] * rank
    if ring == "z":
        at[1], at[3] = lax.rem(position, 2), lax.div(position, 2)
    else:
        at[DIMS[ring][0]] = position
    return at


def positions(ring):
    here = place(ring)
    odd = lax.axis_index("c") * 2
    return here, here ^ (1 + odd), here ^ (3 - odd), here ^ 2


def put_blocks(blocks, positions, ring):
    shape = list(blocks[0].shape)
    for d in DIMS[ring]:
        shape[d] = 4 // len(DIMS[ring])
    out = jnp.zeros(shape, blocks[0].dtype)
    for block, position in zip(blocks, positions):
        out = lax.dynamic_update_slice(out, block, start_at(ring, position, out.ndim))
    return out


def gather(values, rings):
    near = [partner(v, r, 0) for v, r in zip(values, rings)]
    twos = [partner(jnp.stack([v, n]), r, 1) for v, n, r in zip(values, near, rings)]
    return [
        put_blocks([v, n, t[0], t[1]], positions(r), r)
        for v, n, t, r in zip(values, near, twos, rings)
    ]


def gather_wide_start(values, rings):
    near = [partner(v, r, 0) for v, r in zip(values, rings)]
    across = [partner(v, r, 1) for v, r in zip(values, rings)]
    return near, across


def gather_wide_end(values, rings, near, across):
    far = [partner(n, r, 1) for n, r in zip(near, rings)]
    return [
        put_blocks([v, n, a, f], positions(r), r)
        for v, n, a, f, r in zip(values, near, across, far, rings)
    ]


def block_of(array, ring, position):
    shape = list(array.shape)
    for d in DIMS[ring]:
        shape[d] = 1
    return lax.dynamic_slice(array, start_at(ring, position, array.ndim), shape)


def blocks_of(array, ring):
    own, near, across, far = (block_of(array, ring, p) for p in positions(ring))
    return own, near, jnp.stack([across, far])


def sum_start(blocks, rings):
    return [partner(v[2], r, 1) for v, r in zip(blocks, rings)]


def sum_middle(blocks, rings, twos):
    return [
        partner((v[1].astype(f32) + t[1].astype(f32)).astype(bf), r, 0)
        for v, r, t in zip(blocks, rings, twos)
    ]


def sum_end(blocks, twos, ones):
    return [
        v[0].astype(f32) + t[0].astype(f32) + n.astype(f32) for v, t, n in zip(blocks, twos, ones)
    ]


def sum_over(arrays, rings):
    blocks = [blocks_of(v, r) for v, r in zip(arrays, rings)]
    twos = sum_start(blocks, rings)
    return sum_end(blocks, twos, sum_middle(blocks, rings, twos))


def matmul(left, right):
    return jnp.dot(left, right, preferred_element_type=f32)


def outer_sum(left, right):
    return lax.dot_general(
        left, right, (((0,), (0,)), ((), ())), preferred_element_type=f32
    )


def times_transpose(grad, weight):
    return lax.dot_general(
        grad, weight, (((1,), (1,)), ((), ())), preferred_element_type=f32
    )


def feed_forward_kernel(
    place_ref, h_ref, g_ref, wg_ref, wu_ref, wd_ref, out_ref, dh_ref, gd_ref, *refs
):
    grad_refs, (turned_ref, hg_ref, hu_ref) = refs[:4], refs[4:]

    @pl.when(pl.program_id(0) == 0)
    def _():
        out_ref[...] = jnp.zeros_like(out_ref)
        dh_ref[...] = jnp.zeros_like(dh_ref)
        turned_ref[...] = h_ref[...].T
        for k in range(4):
            at = pl.multiple_of(place_ref[k] * 256, 256)
            hg_ref[k * 256 : (k + 1) * 256] = turned_ref[pl.ds(at, 256)]
            low, high = lax.rem(place_ref[4 + k], 2), lax.div(place_ref[4 + k], 2)
            for x in range(4):
                for y in range(4):
                    at = pl.multiple_of((((x * 2 + low) * 4 + y) * 2 + high) * 16, 16)
                    to = k * 256 + (x * 4 + y) * 16
                    hu_ref[to : to + 16] = turned_ref[pl.ds(at, 16)]

    h, g, wg, wu, wd = h_ref[...], g_ref[...], wg_ref[...], wu_ref[...], wd_ref[...]
    gate = matmul(h, wg)
    up = matmul(h, wu)
    d_hidden = times_transpose(g, wd)
    sigma = jax.nn.sigmoid(gate)
    swish = gate * sigma
    hidden = (swish * up).astype(bf)
    d_gate = (d_hidden * up * sigma * (1.0 + gate * (1.0 - sigma))).astype(bf)
    d_up = (d_hidden * swish).astype(bf)
    gd_ref[...] = outer_sum(hidden, g).astype(bf)
    block = hg_ref.shape[0] // 4
    for h_turned, grad, refs in ((hg_ref, d_gate, grad_refs[:2]), (hu_ref, d_up, grad_refs[2:])):
        for k in range(4):
            part = matmul(h_turned[k * block : (k + 1) * block], grad)
            refs[k // 2][k % 2] = part.astype(bf)
    out_ref[...] += matmul(hidden, wd)
    dh_ref[...] += times_transpose(d_gate, wg) + times_transpose(d_up, wu)


def feed_forward(places, h, g, wg, wu, wd):
    rows, width = h.shape
    hidden, tile = wg.shape[1], 256
    whole = pl.BlockSpec((rows, width), lambda i: (0, 0))
    columns = pl.BlockSpec((width, tile), lambda i: (0, i))
    blocks = pl.BlockSpec((2, width // 4, tile), lambda i: (0, 0, i))
    down = pl.BlockSpec((tile, width), lambda i: (i, 0))
    return pl.pallas_call(
        feed_forward_kernel,
        grid=(hidden // tile,),
        in_specs=[
            pl.BlockSpec(memory_space=pltpu.SMEM), whole, whole, columns, columns, down,
        ],
        out_specs=[whole, whole, down] + [blocks] * 4,
        out_shape=[
            jax.ShapeDtypeStruct((rows, width), f32),
            jax.ShapeDtypeStruct((rows, width), f32),
            jax.ShapeDtypeStruct((hidden, width), bf),
        ]
        + [jax.ShapeDtypeStruct((2, width // 4, hidden), bf)] * 4,
        scratch_shapes=[pltpu.VMEM((width, rows), bf)] * 3,
        compiler_params=pltpu.CompilerParams(
            dimension_semantics=("arbitrary",), vmem_limit_bytes=48 * 1024 * 1024
        ),
        cost_estimate=pl.CostEstimate(
            flops=18 * rows * width * hidden,
            bytes_accessed=12 * width * hidden + 16 * rows * width,
            transcendentals=rows * hidden,
        ),
    )(places, h, g, wg, wu, wd)


def local(inputs, w_in, w_out, w_gate, w_up, w_down, conv_weight, gain_a, gain_b, cotangent):
    groups, tokens, width = inputs.shape
    rows = groups * tokens
    hidden = w_gate.shape[1] // 2
    half = width // 2
    quarter = half // 2
    core = lax.axis_index("c")
    first = core == 0

    def in_order(mine, other, axis):
        return jnp.where(
            first,
            jnp.concatenate([mine, other], axis=axis),
            jnp.concatenate([other, mine], axis=axis),
        )

    x_own = inputs.reshape(rows, width)
    g_own = cotangent.reshape(rows, width)
    x_all = jnp.concatenate([x_own, swap(x_own)], axis=0)
    df_own = g_own.astype(bf)
    d_out = jnp.concatenate([df_own, swap(df_own)], axis=0)

    params = jnp.concatenate(
        [gain_a[:, None], gain_b[:, None], conv_weight.T, jnp.zeros((8, 123), f32)], axis=1
    )

    def columns(side):
        def cut(w, at, size):
            return lax.dynamic_slice_in_dim(w, at, size, 1)

        return jnp.concatenate(
            [
                cut(w_gate, side * hidden, hidden),
                cut(w_in, side * half, half),
                cut(w_in, 2 * width + side * half, quarter),
                params,
                cut(w_up, side * hidden, hidden),
                cut(w_in, width + side * half, half),
                cut(w_in, 2 * width + side * half + quarter, quarter),
            ],
            axis=1,
        ).astype(bf)

    shard = in_order(columns(core), swap(columns(1 - core)), 0)
    x_cols = hidden + half + quarter + 128
    x_shard = shard[None, None, None, None, :, :x_cols]
    y_shard = shard[None, None, None, None, :, x_cols:]
    d_shard = trade_halves(jnp.concatenate([w_down, w_out], axis=0).astype(bf))
    n_down, n_out = w_down.shape[0], w_out.shape[0]

    x_part, y_part, d_part = gather(
        [x_shard, y_shard, d_shard[None, None, None, None]], ["z", "y", "x"]
    )

    def pair_up(a):
        a = a.reshape(2, 2, a.shape[-2], width).transpose(1, 0, 2, 3)
        return a.reshape(2, 1, 1, 1, -1, width)

    d_part = jnp.concatenate(
        [pair_up(d_part[..., :n_down, :]), pair_up(d_part[..., n_down:, :])], axis=4
    )
    x_part, y_part, d_part, x_all, d_out = lax.optimization_barrier(
        (x_part, y_part, d_part, x_all, d_out)
    )
    x_part, y_part, d_part = gather([x_part, y_part, d_part], ["y", "x", "z"])
    x_part, y_part, d_part = lax.optimization_barrier((x_part, y_part, d_part))

    last = ["x", "z", "y"]
    ones = [x_part[..., hidden:], y_part[..., hidden:], d_part[..., 2 * n_down :, :]]
    near_one, across_one = gather_wide_start(ones, last)
    near_one = lax.optimization_barrier(near_one)
    ones = gather_wide_end(ones, last, near_one, across_one)
    twos = (x_part[..., :hidden], y_part[..., :hidden], d_part[..., : 2 * n_down, :])
    twos, near_one, across_one = lax.optimization_barrier((twos, near_one, across_one))
    near_two, across_two = gather_wide_start(twos, last)
    x_one, y_one = ones[0].reshape(width, -1), ones[1].reshape(width, -1)
    full_out = ones[2].reshape(half, width)
    in_x = x_one
    in_y = y_one
    vectors = x_one[:, half + quarter :].astype(f32).T
    ga, gb = vectors[0], vectors[1]
    taps = lax.dynamic_slice_in_dim(vectors[2:5], core * half, half, 1)

    scale_a = lax.rsqrt(jnp.mean(x_all * x_all, axis=-1, keepdims=True) + EPS)
    normed = (x_all * scale_a * ga).astype(bf)
    proj_x = matmul(normed, in_x)
    proj_y = matmul(normed, in_y)
    b_part, c_part = proj_x[:, :half], proj_y[:, :half]
    v_part = jnp.concatenate([proj_x[:, half : half + quarter], proj_y[:, half:]], axis=1)
    product = (b_part * v_part).reshape(2, groups, tokens, half)
    product, near_two = lax.optimization_barrier((product, near_two))
    twos = gather_wide_end(twos, last, near_two, across_two)
    full_gate, full_up = twos[0].reshape(width, hidden), twos[1].reshape(width, hidden)
    full_down = twos[2].reshape(hidden, width)


    def along_sequence(value, steps):
        chips = 8
        return lax.ppermute(
            value,
            ("y", "zh"),
            [(i, i + steps) for i in range(chips) if 0 <= i + steps < chips],
        )

    tail_own, tail_other = product[0, :, tokens - 2 :], product[1, :, tokens - 2 :]
    halo = along_sequence(jnp.where(first, tail_other, tail_own), 1)
    before = jnp.stack(
        [jnp.where(first, halo, tail_other), jnp.where(first, tail_own, halo)]
    )
    extended = jnp.concatenate([before, product], axis=2)
    conv_out = (
        taps[0] * extended[:, :, :-2] + taps[1] * extended[:, :, 1:-1] + taps[2] * extended[:, :, 2:]
    ).reshape(2 * rows, half)
    gated = (c_part * conv_out).astype(bf)
    def sum_cores(partial):
        return partial[:rows] + swap(partial[rows:])

    middle = x_own + sum_cores(matmul(gated, full_out))
    scale_b = lax.rsqrt(jnp.mean(middle * middle, axis=-1, keepdims=True) + EPS)
    normed_b_own = (middle * scale_b * gb).astype(bf)
    normed_b = jnp.concatenate([normed_b_own, swap(normed_b_own)], axis=0)
    chips = (4, 2, 4, 2)
    places = jnp.stack([*positions("x"), *positions("z")])
    out_part, dh_part, grad_w_down, gate_keep, gate_send, up_keep, up_send = feed_forward(
        places, normed_b, d_out, full_gate, full_up, full_down
    )

    gate_keep, gate_send = (v.reshape(2, 1, 2, 4, 2, 16, hidden) for v in (gate_keep, gate_send))
    up_keep, up_send = (v.reshape(2, 4, 1, 4, 1, 16, hidden) for v in (up_keep, up_send))
    grads_two = [
        (gate_keep[0], gate_keep[1], gate_send),
        (up_keep[0], up_keep[1], up_send),
        blocks_of(grad_w_down.reshape(2, 2, 4, 2, 2 * n_down, width), "y"),
    ]
    arrived_two = sum_start(grads_two, last)

    d_normed_b = sum_cores(dh_part)
    grad_gain_b = jnp.sum(d_normed_b * middle * scale_b, axis=0)
    scaled_b = d_normed_b * gb
    d_middle = (
        g_own
        + scale_b * scaled_b
        - middle * scale_b**3 * jnp.mean(scaled_b * middle, axis=-1, keepdims=True)
    )
    d_branch_own = d_middle.astype(bf)
    d_branch = jnp.concatenate([d_branch_own, swap(d_branch_own)], axis=0)
    grad_w_out = outer_sum(gated, d_branch).astype(bf)
    d_gated = times_transpose(d_branch, full_out)
    d_c = d_gated * conv_out
    d_conv = (d_gated * c_part).reshape(2, groups, tokens, half)
    head_own, head_other = d_conv[0, :, :2], d_conv[1, :, :2]
    halo_b = along_sequence(jnp.where(first, head_own, head_other), -1)
    after = jnp.stack(
        [jnp.where(first, head_other, halo_b), jnp.where(first, halo_b, head_own)]
    )
    ext_b = jnp.concatenate([d_conv, after], axis=2)
    d_product = (
        taps[0] * ext_b[:, :, 2:] + taps[1] * ext_b[:, :, 1:-1] + taps[2] * ext_b[:, :, :-2]
    ).reshape(2 * rows, half)
    grad_taps = jnp.stack(
        [jnp.sum(d_conv * extended[:, :, k : k + tokens], axis=(0, 1, 2)) for k in range(3)]
    )
    d_v = d_product * b_part
    d_x = jnp.concatenate(
        [d_product * v_part, d_v[:, :quarter], jnp.zeros((2 * rows, 128), f32)], axis=1
    ).astype(bf)
    d_y = jnp.concatenate([d_c, d_v[:, quarter:]], axis=1).astype(bf)
    d_x, d_y, arrived_two = lax.optimization_barrier((d_x, d_y, arrived_two))
    arrived_one = sum_middle(grads_two, last, arrived_two)
    grad_in_x = outer_sum(normed, d_x).astype(bf)
    grad_in_y = outer_sum(normed, d_y).astype(bf)
    d_normed_part = times_transpose(d_x, in_x) + times_transpose(d_y, in_y)
    grad_gain_a = jnp.sum(d_normed_part * x_all * scale_a, axis=0)
    d_normed = sum_cores(d_normed_part)
    scale_own = scale_a[:rows]
    scaled_a = d_normed * ga
    grad_rows = (
        d_middle
        + scale_own * scaled_a
        - x_own * scale_own**3 * jnp.mean(scaled_a * x_own, axis=-1, keepdims=True)
    )

    both_taps = lax.dynamic_update_slice(jnp.zeros((3, width), f32), grad_taps, (0, core * half))
    grad_vectors = jnp.concatenate(
        [grad_gain_a[None], grad_gain_b[None], both_taps, jnp.zeros((123, width), f32)], axis=0
    ).astype(bf)
    grad_x_one = lax.dynamic_update_slice(grad_in_x, grad_vectors.T, (0, half + quarter))
    grads_one = [
        grad_x_one.reshape(*chips, 16, -1),
        grad_in_y.reshape(*chips, 16, -1),
        grad_w_out.reshape(2, 2, 4, 2, 2 * n_out, width),
    ]
    sums_two = sum_end(grads_two, arrived_two, arrived_one)
    sums_one = sum_over(grads_one, last)
    x_sum, y_sum, d_sum = sum_over(
        [
            jnp.concatenate(v, axis=a).astype(bf)
            for *v, a in zip(sums_two, sums_one, (-1, -1, -2))
        ],
        ["y", "x", "z"],
    )

    def unpair(a):
        a = a.reshape(2, 2, -1, width).transpose(1, 0, 2, 3)
        return a.reshape(4, 1, 1, 1, -1, width)

    d_sum = jnp.concatenate(
        [unpair(d_sum[..., : 2 * n_down, :]), unpair(d_sum[..., 2 * n_down :, :])], axis=4
    )
    x_sum, y_sum, d_sum = sum_over(
        [x_sum.astype(bf), y_sum.astype(bf), d_sum.astype(bf)], ["z", "y", "x"]
    )
    d_sum = trade_halves(d_sum.reshape(n_down + n_out, width))

    sums = jnp.concatenate([x_sum.reshape(16, -1), y_sum.reshape(16, -1)], axis=-1)
    mine = lax.dynamic_slice_in_dim(sums, core * 8, 8, 0)
    other = swap(lax.dynamic_slice_in_dim(sums, (1 - core) * 8, 8, 0))

    def cut(a, at, size):
        return a[:, at : at + size]

    def joined(at, size):
        return in_order(cut(mine, at, size), cut(other, at, size), 1)

    at_v1, at_vec = hidden + half, hidden + half + quarter
    at_up, at_c, at_v2 = x_cols, x_cols + hidden, x_cols + hidden + half
    v_mine = jnp.concatenate([cut(mine, at_v1, quarter), cut(mine, at_v2, quarter)], axis=1)
    v_other = jnp.concatenate([cut(other, at_v1, quarter), cut(other, at_v2, quarter)], axis=1)
    grad_w_in = jnp.concatenate(
        [joined(hidden, half), joined(at_c, half), in_order(v_mine, v_other, 1)], axis=1
    )
    vec = (cut(mine, at_vec, 128) + cut(other, at_vec, 128))[:, :5].T
    outputs = middle + sum_cores(out_part)
    return (
        outputs.reshape(groups, tokens, width),
        grad_rows.reshape(groups, tokens, width),
        grad_w_in,
        d_sum[n_down:],
        joined(0, hidden),
        joined(at_up, hidden),
        d_sum[:n_down],
        vec[2:5],
        vec[0],
        vec[1],
    )


def solution(mesh):
    fine = Mesh(mesh.devices.reshape(SIZES), AXES)
    dp, seq = ("x", "zl"), ("y", "zh", "c")
    tokens = P(dp, seq, None)
    by_row = P(AXES, None)
    vector = P(AXES)
    taps = P(None, AXES)
    return jax.shard_map(
        local,
        mesh=fine,
        in_specs=(
            tokens, by_row, by_row, by_row, by_row, by_row, taps, vector, vector, tokens,
        ),
        out_specs=(
            tokens, tokens, by_row, by_row, by_row, by_row, by_row, taps, vector, vector,
        ),
        check_vma=False,
    )
```

```python
import jax
import jax.numpy as jnp
from jax import lax
from jax.experimental import pallas as pl
from jax.experimental.pallas import tpu as pltpu
from jax.sharding import Mesh, PartitionSpec as P

AXES = ("x", "zl", "y", "zh", "c")
SIZES = (4, 2, 4, 2, 2)
EPS = 1e-05
bf = jnp.bfloat16
f32 = jnp.float32

RING_AXES = {"x": ("x",), "y": ("y",), "z": ("zl", "zh")}
SLOT = {"x": (0, 1, 2, 3), "y": (0, 1, 2, 3), "z": (0, 2, 1, 3)}
DIMS = {"x": (0,), "y": (2,), "z": (1, 3)}


def swap(value):
    return lax.ppermute(value, "c", [(0, 1), (1, 0)])


def partner(value, ring, step):
    slot = SLOT[ring]
    masks = (1, 3) if step == 0 else (3, 1)
    pairs = [(2 * slot[i] + c, 2 * slot[i ^ masks[c]] + c) for i in range(4) for c in range(2)]
    return lax.ppermute(value, (*RING_AXES[ring], "c"), pairs)


def trade_halves(value):
    return lax.ppermute(
        value, ("x", "c"), [(0, 0), (1, 4), (2, 2), (3, 6), (4, 1), (5, 5), (6, 3), (7, 7)]
    )


def place(ring):
    if ring == "z":
        return 2 * lax.axis_index("zh") + lax.axis_index("zl")
    return lax.axis_index(ring)


def start_at(ring, position, rank):
    at = [0] * rank
    if ring == "z":
        at[1], at[3] = lax.rem(position, 2), lax.div(position, 2)
    else:
        at[DIMS[ring][0]] = position
    return at


def positions(ring):
    here = place(ring)
    odd = lax.axis_index("c") * 2
    return here, here ^ (1 + odd), here ^ (3 - odd), here ^ 2


def put_blocks(blocks, positions, ring):
    shape = list(blocks[0].shape)
    for d in DIMS[ring]:
        shape[d] = 4 // len(DIMS[ring])
    out = jnp.zeros(shape, blocks[0].dtype)
    for block, position in zip(blocks, positions):
        out = lax.dynamic_update_slice(out, block, start_at(ring, position, out.ndim))
    return out


def gather(values, rings):
    near = [partner(v, r, 0) for v, r in zip(values, rings)]
    twos = [partner(jnp.stack([v, n]), r, 1) for v, n, r in zip(values, near, rings)]
    return [
        put_blocks([v, n, t[0], t[1]], positions(r), r)
        for v, n, t, r in zip(values, near, twos, rings)
    ]


def gather_wide_start(values, rings):
    near = [partner(v, r, 0) for v, r in zip(values, rings)]
    across = [partner(v, r, 1) for v, r in zip(values, rings)]
    return near, across


def gather_wide_end(values, rings, near, across):
    far = [partner(n, r, 1) for n, r in zip(near, rings)]
    return [
        put_blocks([v, n, a, f], positions(r), r)
        for v, n, a, f, r in zip(values, near, across, far, rings)
    ]


def block_of(array, ring, position):
    shape = list(array.shape)
    for d in DIMS[ring]:
        shape[d] = 1
    return lax.dynamic_slice(array, start_at(ring, position, array.ndim), shape)


def blocks_of(array, ring):
    own, near, across, far = (block_of(array, ring, p) for p in positions(ring))
    return own, near, jnp.stack([across, far])


def sum_start(blocks, rings):
    return [partner(v[2], r, 1) for v, r in zip(blocks, rings)]


def sum_middle(blocks, rings, twos):
    return [
        partner((v[1].astype(f32) + t[1].astype(f32)).astype(bf), r, 0)
        for v, r, t in zip(blocks, rings, twos)
    ]


def sum_end(blocks, twos, ones):
    return [
        v[0].astype(f32) + t[0].astype(f32) + n.astype(f32) for v, t, n in zip(blocks, twos, ones)
    ]


def sum_over(arrays, rings):
    blocks = [blocks_of(v, r) for v, r in zip(arrays, rings)]
    twos = sum_start(blocks, rings)
    return sum_end(blocks, twos, sum_middle(blocks, rings, twos))


def matmul(left, right):
    return jnp.dot(left, right, preferred_element_type=f32)


def outer_sum(left, right):
    return lax.dot_general(
        left, right, (((0,), (0,)), ((), ())), preferred_element_type=f32
    )


def times_transpose(grad, weight):
    return lax.dot_general(
        grad, weight, (((1,), (1,)), ((), ())), preferred_element_type=f32
    )


def feed_forward_kernel(
    place_ref, h_ref, g_ref, wg_ref, wu_ref, wd_ref, out_ref, dh_ref, gd_ref, *refs
):
    grad_refs, (turned_ref, hg_ref, hu_ref) = refs[:4], refs[4:]

    @pl.when(pl.program_id(0) == 0)
    def _():
        out_ref[...] = jnp.zeros_like(out_ref)
        dh_ref[...] = jnp.zeros_like(dh_ref)
        turned_ref[...] = h_ref[...].T
        for k in range(4):
            at = pl.multiple_of(place_ref[k] * 256, 256)
            hg_ref[k * 256 : (k + 1) * 256] = turned_ref[pl.ds(at, 256)]
            low, high = lax.rem(place_ref[4 + k], 2), lax.div(place_ref[4 + k], 2)
            for x in range(4):
                for y in range(4):
                    at = pl.multiple_of((((x * 2 + low) * 4 + y) * 2 + high) * 16, 16)
                    to = k * 256 + (x * 4 + y) * 16
                    hu_ref[to : to + 16] = turned_ref[pl.ds(at, 16)]

    h, g, wg, wu, wd = h_ref[...], g_ref[...], wg_ref[...], wu_ref[...], wd_ref[...]
    gate = matmul(h, wg)
    up = matmul(h, wu)
    d_hidden = times_transpose(g, wd)
    sigma = jax.nn.sigmoid(gate)
    swish = gate * sigma
    hidden = (swish * up).astype(bf)
    d_gate = (d_hidden * up * sigma * (1.0 + gate * (1.0 - sigma))).astype(bf)
    d_up = (d_hidden * swish).astype(bf)
    gd_ref[...] = outer_sum(hidden, g).astype(bf)
    block = hg_ref.shape[0] // 4
    for h_turned, grad, refs in ((hg_ref, d_gate, grad_refs[:2]), (hu_ref, d_up, grad_refs[2:])):
        for k in range(4):
            part = matmul(h_turned[k * block : (k + 1) * block], grad)
            refs[k // 2][k % 2] = part.astype(bf)
    out_ref[...] += matmul(hidden, wd)
    dh_ref[...] += times_transpose(d_gate, wg) + times_transpose(d_up, wu)


def feed_forward(places, h, g, wg, wu, wd):
    rows, width = h.shape
    hidden, tile = wg.shape[1], 256
    whole = pl.BlockSpec((rows, width), lambda i: (0, 0))
    columns = pl.BlockSpec((width, tile), lambda i: (0, i))
    blocks = pl.BlockSpec((2, width // 4, tile), lambda i: (0, 0, i))
    down = pl.BlockSpec((tile, width), lambda i: (i, 0))
    return pl.pallas_call(
        feed_forward_kernel,
        grid=(hidden // tile,),
        in_specs=[
            pl.BlockSpec(memory_space=pltpu.SMEM), whole, whole, columns, columns, down,
        ],
        out_specs=[whole, whole, down] + [blocks] * 4,
        out_shape=[
            jax.ShapeDtypeStruct((rows, width), f32),
            jax.ShapeDtypeStruct((rows, width), f32),
            jax.ShapeDtypeStruct((hidden, width), bf),
        ]
        + [jax.ShapeDtypeStruct((2, width // 4, hidden), bf)] * 4,
        scratch_shapes=[pltpu.VMEM((width, rows), bf)] * 3,
        compiler_params=pltpu.CompilerParams(
            dimension_semantics=("arbitrary",), vmem_limit_bytes=48 * 1024 * 1024
        ),
        cost_estimate=pl.CostEstimate(
            flops=18 * rows * width * hidden,
            bytes_accessed=12 * width * hidden + 16 * rows * width,
            transcendentals=rows * hidden,
        ),
    )(places, h, g, wg, wu, wd)


def local(inputs, w_in, w_out, w_gate, w_up, w_down, conv_weight, gain_a, gain_b, cotangent):
    groups, tokens, width = inputs.shape
    rows = groups * tokens
    hidden = w_gate.shape[1] // 2
    half = width // 2
    quarter = half // 2
    core = lax.axis_index("c")
    first = core == 0

    def in_order(mine, other, axis):
        return jnp.where(
            first,
            jnp.concatenate([mine, other], axis=axis),
            jnp.concatenate([other, mine], axis=axis),
        )

    x_own = inputs.reshape(rows, width)
    g_own = cotangent.reshape(rows, width)
    x_all = jnp.concatenate([x_own, swap(x_own)], axis=0)
    df_own = g_own.astype(bf)
    d_out = jnp.concatenate([df_own, swap(df_own)], axis=0)

    params = jnp.concatenate(
        [gain_a[:, None], gain_b[:, None], conv_weight.T, jnp.zeros((8, 123), f32)], axis=1
    )

    def columns(side):
        def cut(w, at, size):
            return lax.dynamic_slice_in_dim(w, at, size, 1)

        return jnp.concatenate(
            [
                cut(w_gate, side * hidden, hidden),
                cut(w_in, side * half, half),
                cut(w_in, 2 * width + side * half, quarter),
                params,
                cut(w_up, side * hidden, hidden),
                cut(w_in, width + side * half, half),
                cut(w_in, 2 * width + side * half + quarter, quarter),
            ],
            axis=1,
        ).astype(bf)

    shard = in_order(columns(core), swap(columns(1 - core)), 0)
    x_cols = hidden + half + quarter + 128
    x_shard = shard[None, None, None, None, :, :x_cols]
    y_shard = shard[None, None, None, None, :, x_cols:]
    d_shard = trade_halves(jnp.concatenate([w_down, w_out], axis=0).astype(bf))
    n_down, n_out = w_down.shape[0], w_out.shape[0]

    x_part, y_part, d_part = gather(
        [x_shard, y_shard, d_shard[None, None, None, None]], ["z", "y", "x"]
    )

    def pair_up(a):
        a = a.reshape(2, 2, a.shape[-2], width).transpose(1, 0, 2, 3)
        return a.reshape(2, 1, 1, 1, -1, width)

    d_part = jnp.concatenate(
        [pair_up(d_part[..., :n_down, :]), pair_up(d_part[..., n_down:, :])], axis=4
    )
    x_part, y_part, d_part, x_all, d_out = lax.optimization_barrier(
        (x_part, y_part, d_part, x_all, d_out)
    )
    middle_rings = ["y", "x", "z"]
    parts = [x_part, y_part, d_part]
    near, across = gather_wide_start(parts, middle_rings)
    x_part, y_part, d_part = gather_wide_end(parts, middle_rings, near, across)
    x_part, y_part, d_part = lax.optimization_barrier((x_part, y_part, d_part))

    last = ["x", "z", "y"]
    ones = [x_part[..., hidden:], y_part[..., hidden:], d_part[..., 2 * n_down :, :]]
    near_one, across_one = gather_wide_start(ones, last)
    near_one = lax.optimization_barrier(near_one)
    ones = gather_wide_end(ones, last, near_one, across_one)
    twos = (x_part[..., :hidden], y_part[..., :hidden], d_part[..., : 2 * n_down, :])
    twos, near_one, across_one = lax.optimization_barrier((twos, near_one, across_one))
    near_two, across_two = gather_wide_start(twos, last)
    x_one, y_one = ones[0].reshape(width, -1), ones[1].reshape(width, -1)
    full_out = ones[2].reshape(half, width)
    in_x = x_one
    in_y = y_one
    vectors = x_one[:, half + quarter :].astype(f32).T
    ga, gb = vectors[0], vectors[1]
    taps = lax.dynamic_slice_in_dim(vectors[2:5], core * half, half, 1)

    scale_a = lax.rsqrt(jnp.mean(x_all * x_all, axis=-1, keepdims=True) + EPS)
    normed = (x_all * scale_a * ga).astype(bf)
    proj_x = matmul(normed, in_x)
    proj_y = matmul(normed, in_y)
    b_part, c_part = proj_x[:, :half], proj_y[:, :half]
    v_part = jnp.concatenate([proj_x[:, half : half + quarter], proj_y[:, half:]], axis=1)
    product = (b_part * v_part).reshape(2, groups, tokens, half)
    product, near_two = lax.optimization_barrier((product, near_two))
    twos = gather_wide_end(twos, last, near_two, across_two)
    full_gate, full_up = twos[0].reshape(width, hidden), twos[1].reshape(width, hidden)
    full_down = twos[2].reshape(hidden, width)


    def along_sequence(value, steps):
        chips = 8
        return lax.ppermute(
            value,
            ("y", "zh"),
            [(i, i + steps) for i in range(chips) if 0 <= i + steps < chips],
        )

    tail_own, tail_other = product[0, :, tokens - 2 :], product[1, :, tokens - 2 :]
    halo = along_sequence(jnp.where(first, tail_other, tail_own), 1)
    before = jnp.stack(
        [jnp.where(first, halo, tail_other), jnp.where(first, tail_own, halo)]
    )
    extended = jnp.concatenate([before, product], axis=2)
    conv_out = (
        taps[0] * extended[:, :, :-2] + taps[1] * extended[:, :, 1:-1] + taps[2] * extended[:, :, 2:]
    ).reshape(2 * rows, half)
    gated = (c_part * conv_out).astype(bf)
    def sum_cores(partial):
        return partial[:rows] + swap(partial[rows:])

    middle = x_own + sum_cores(matmul(gated, full_out))
    scale_b = lax.rsqrt(jnp.mean(middle * middle, axis=-1, keepdims=True) + EPS)
    normed_b_own = (middle * scale_b * gb).astype(bf)
    normed_b = jnp.concatenate([normed_b_own, swap(normed_b_own)], axis=0)
    chips = (4, 2, 4, 2)
    places = jnp.stack([*positions("x"), *positions("z")])
    out_part, dh_part, grad_w_down, gate_keep, gate_send, up_keep, up_send = feed_forward(
        places, normed_b, d_out, full_gate, full_up, full_down
    )

    gate_keep, gate_send = (v.reshape(2, 1, 2, 4, 2, 16, hidden) for v in (gate_keep, gate_send))
    up_keep, up_send = (v.reshape(2, 4, 1, 4, 1, 16, hidden) for v in (up_keep, up_send))
    grads_two = [
        (gate_keep[0], gate_keep[1], gate_send),
        (up_keep[0], up_keep[1], up_send),
        blocks_of(grad_w_down.reshape(2, 2, 4, 2, 2 * n_down, width), "y"),
    ]
    arrived_two = sum_start(grads_two, last)

    d_normed_b = sum_cores(dh_part)
    grad_gain_b = jnp.sum(d_normed_b * middle * scale_b, axis=0)
    scaled_b = d_normed_b * gb
    d_middle = (
        g_own
        + scale_b * scaled_b
        - middle * scale_b**3 * jnp.mean(scaled_b * middle, axis=-1, keepdims=True)
    )
    d_branch_own = d_middle.astype(bf)
    d_branch = jnp.concatenate([d_branch_own, swap(d_branch_own)], axis=0)
    grad_w_out = outer_sum(gated, d_branch).astype(bf)
    d_gated = times_transpose(d_branch, full_out)
    d_c = d_gated * conv_out
    d_conv = (d_gated * c_part).reshape(2, groups, tokens, half)
    head_own, head_other = d_conv[0, :, :2], d_conv[1, :, :2]
    halo_b = along_sequence(jnp.where(first, head_own, head_other), -1)
    after = jnp.stack(
        [jnp.where(first, head_other, halo_b), jnp.where(first, halo_b, head_own)]
    )
    ext_b = jnp.concatenate([d_conv, after], axis=2)
    d_product = (
        taps[0] * ext_b[:, :, 2:] + taps[1] * ext_b[:, :, 1:-1] + taps[2] * ext_b[:, :, :-2]
    ).reshape(2 * rows, half)
    grad_taps = jnp.stack(
        [jnp.sum(d_conv * extended[:, :, k : k + tokens], axis=(0, 1, 2)) for k in range(3)]
    )
    d_v = d_product * b_part
    d_x = jnp.concatenate(
        [d_product * v_part, d_v[:, :quarter], jnp.zeros((2 * rows, 128), f32)], axis=1
    ).astype(bf)
    d_y = jnp.concatenate([d_c, d_v[:, quarter:]], axis=1).astype(bf)
    d_x, d_y, arrived_two = lax.optimization_barrier((d_x, d_y, arrived_two))
    arrived_one = sum_middle(grads_two, last, arrived_two)
    grad_in_x = outer_sum(normed, d_x).astype(bf)
    grad_in_y = outer_sum(normed, d_y).astype(bf)
    d_normed_part = times_transpose(d_x, in_x) + times_transpose(d_y, in_y)
    grad_gain_a = jnp.sum(d_normed_part * x_all * scale_a, axis=0)
    d_normed = sum_cores(d_normed_part)
    scale_own = scale_a[:rows]
    scaled_a = d_normed * ga
    grad_rows = (
        d_middle
        + scale_own * scaled_a
        - x_own * scale_own**3 * jnp.mean(scaled_a * x_own, axis=-1, keepdims=True)
    )

    both_taps = lax.dynamic_update_slice(jnp.zeros((3, width), f32), grad_taps, (0, core * half))
    grad_vectors = jnp.concatenate(
        [grad_gain_a[None], grad_gain_b[None], both_taps, jnp.zeros((123, width), f32)], axis=0
    ).astype(bf)
    grad_x_one = lax.dynamic_update_slice(grad_in_x, grad_vectors.T, (0, half + quarter))
    grads_one = [
        grad_x_one.reshape(*chips, 16, -1),
        grad_in_y.reshape(*chips, 16, -1),
        grad_w_out.reshape(2, 2, 4, 2, 2 * n_out, width),
    ]
    sums_two = sum_end(grads_two, arrived_two, arrived_one)
    sums_one = sum_over(grads_one, last)
    x_sum, y_sum, d_sum = sum_over(
        [
            jnp.concatenate(v, axis=a).astype(bf)
            for *v, a in zip(sums_two, sums_one, (-1, -1, -2))
        ],
        ["y", "x", "z"],
    )

    def unpair(a):
        a = a.reshape(2, 2, -1, width).transpose(1, 0, 2, 3)
        return a.reshape(4, 1, 1, 1, -1, width)

    d_sum = jnp.concatenate(
        [unpair(d_sum[..., : 2 * n_down, :]), unpair(d_sum[..., 2 * n_down :, :])], axis=4
    )
    x_sum, y_sum, d_sum = sum_over(
        [x_sum.astype(bf), y_sum.astype(bf), d_sum.astype(bf)], ["z", "y", "x"]
    )
    d_sum = trade_halves(d_sum.reshape(n_down + n_out, width))

    sums = jnp.concatenate([x_sum.reshape(16, -1), y_sum.reshape(16, -1)], axis=-1)
    mine = lax.dynamic_slice_in_dim(sums, core * 8, 8, 0)
    other = swap(lax.dynamic_slice_in_dim(sums, (1 - core) * 8, 8, 0))

    def cut(a, at, size):
        return a[:, at : at + size]

    def joined(at, size):
        return in_order(cut(mine, at, size), cut(other, at, size), 1)

    at_v1, at_vec = hidden + half, hidden + half + quarter
    at_up, at_c, at_v2 = x_cols, x_cols + hidden, x_cols + hidden + half
    v_mine = jnp.concatenate([cut(mine, at_v1, quarter), cut(mine, at_v2, quarter)], axis=1)
    v_other = jnp.concatenate([cut(other, at_v1, quarter), cut(other, at_v2, quarter)], axis=1)
    grad_w_in = jnp.concatenate(
        [joined(hidden, half), joined(at_c, half), in_order(v_mine, v_other, 1)], axis=1
    )
    vec = (cut(mine, at_vec, 128) + cut(other, at_vec, 128))[:, :5].T
    outputs = middle + sum_cores(out_part)
    return (
        outputs.reshape(groups, tokens, width),
        grad_rows.reshape(groups, tokens, width),
        grad_w_in,
        d_sum[n_down:],
        joined(0, hidden),
        joined(at_up, hidden),
        d_sum[:n_down],
        vec[2:5],
        vec[0],
        vec[1],
    )


def solution(mesh):
    fine = Mesh(mesh.devices.reshape(SIZES), AXES)
    dp, seq = ("x", "zl"), ("y", "zh", "c")
    tokens = P(dp, seq, None)
    by_row = P(AXES, None)
    vector = P(AXES)
    taps = P(None, AXES)
    return jax.shard_map(
        local,
        mesh=fine,
        in_specs=(
            tokens, by_row, by_row, by_row, by_row, by_row, taps, vector, vector, tokens,
        ),
        out_specs=(
            tokens, tokens, by_row, by_row, by_row, by_row, by_row, taps, vector, vector,
        ),
        check_vma=False,
    )
```
